512 devices in a mesh: replica: 16 (over x, y_lo), shard: 32 (over y_hi, z, core).
Axes of the slice: x: 4, y: 8 (y_hi: 2, y_lo: 4; y = y_hi * 4 + y_lo), z: 8, core: 2. Of those that a mesh axis runs over, the one named last changes fastest.
Arguments:
- tokens: bfloat16 [65536, 8192], P(('replica', 'shard')), may hold values from -6 to 6
- cotangent: bfloat16 [65536, 512], P(('replica', 'shard')), may hold values from -6 to 6
- biased: float32 [16, 8192, 512], P('replica', 'shard'), may hold values from -0.0625 to 0.0625
- momentum: float32 [16, 8192, 512], P('replica', 'shard'), may hold values from -0.12 to 0.12
- weight: float32 [16], P('replica'), may hold values from 0.25 to 4
- round_index: int32 [1], replicated, may hold values from 0 to 999999
Outputs:
- projected: bfloat16 [65536, 512], P(('replica', 'shard'))
- mixed: float32 [16, 8192, 512], P('replica', 'shard')
- weight_out: float32 [16], P('replica')
- velocity: float32 [16, 8192, 512], P('replica', 'shard')
- debiased: float32 [16, 8192, 512], P('replica', 'shard')
The draws below stay inside these ranges and needn't reach their ends.
Inputs may be any that keep to these rules, and one draw needn't show every extreme that they name: `round_index`: any round number.
All inputs are finite; a program needn't handle non-finite values.
Results may differ from the reference program's by a relative error of at most 0.005.
Values may be sent and summed in bfloat16 or wider, within the bound.
No kernel may reach another device: no remote copies, remote signals or barrier semaphores. Data moves between devices by JAX's collectives and lax.ppermute only.
A program may use at most 64 MiB of HBM per device.

```python
import math
import jax
import jax.numpy as jnp
from jax import lax

D = 8192
KV = 512
REP_TOK = 4096
TOKENS = 65536
HOPS = 4
N_REPLICA = 16


def steps_of(stream_key, shape, shards, low, top_value):
    def one(position, parts):
        heights = jax.random.uniform(jax.random.fold_in(jax.random.fold_in(stream_key, 6), position), (parts,), jnp.float32, low / len(shards), top_value / len(shards))
        return jnp.repeat(jnp.exp(heights), shape[position] // parts).reshape((-1,) + (1,) * (len(shape) - position - 1))

    gain = one(*shards[0])
    for cut in shards[1:]:
        gain = gain * one(*cut)
    return gain


def gaussian(key, dims, deviation, reach, split=(), kind=jnp.bfloat16):
    level = steps_of(key, dims, split, -0.22, 0.18) if split else 1.0
    drawn = jax.random.normal(key, dims, jnp.float32) * deviation * level
    return jnp.minimum(jnp.maximum(drawn, -reach), reach).astype(kind)


def setup_inputs(seed: int = 0) -> dict:
    streams_of = jax.random.split(jax.random.key(seed), 7)
    return {
        "tokens": gaussian(streams_of[0], (TOKENS, D), 1.0, 6.0, ((0, 512),)),
        "cotangent": gaussian(streams_of[1], (TOKENS, KV), 1.0, 6.0, ((0, 512),)),
        "biased": gaussian(streams_of[2], (N_REPLICA, D, KV), D ** -0.5, 0.0625, ((0, 16), (1, 32)), jnp.float32),
        "momentum": gaussian(streams_of[3], (N_REPLICA, D, KV), 0.02, 0.12, ((0, 16), (1, 32)), jnp.float32),
        "weight": jnp.clip(jnp.exp(math.log(4.0) - 2.7725887 * jax.random.uniform(streams_of[4], (N_REPLICA,), jnp.float32) ** steps_of(streams_of[4], (N_REPLICA,), ((0, 16),), -0.2, 0.2)), 0.25, 4.0),
        "round_index": jax.random.randint(streams_of[5], (1,), 0, 1000000).astype(jnp.int32),
    }


MOMENT = 0.9
LEARN = 0.5


def reference(tokens, cotangent, biased, momentum, weight, round_index):
    tok_rep = tokens.reshape(N_REPLICA, REP_TOK, D)
    cot_rep = cotangent.reshape(N_REPLICA, REP_TOK, KV)

    def replica_work(items):
        rows, cots, numer, veloc, scale = items
        current = (numer / scale).astype(jnp.bfloat16)
        output = jnp.dot(rows, current, preferred_element_type=jnp.float32).astype(jnp.bfloat16)
        gradient = lax.dot_general(rows, cots, (((0,), (0,)), ((), ())), preferred_element_type=jnp.float32) / REP_TOK
        new_veloc = MOMENT * veloc + gradient
        stepped = numer - LEARN * (gradient + MOMENT * new_veloc)
        return output, stepped, new_veloc

    output, stepped, velocity = lax.map(replica_work, (tok_rep, cot_rep, biased, momentum, weight))
    power = (round_index[0] % HOPS).astype(jnp.int32)
    dist = jnp.left_shift(jnp.int32(1), power)
    source = (jnp.arange(N_REPLICA, dtype=jnp.int32) - dist) % N_REPLICA
    mixed = 0.5 * (stepped + stepped[source])
    weight_out = 0.5 * (weight + weight[source])
    debiased = mixed / weight_out[:, None, None]
    return output.reshape(TOKENS, KV), mixed, weight_out, velocity, debiased
```

```python
from functools import partial

import jax
import jax.numpy as jnp
from jax import lax
from jax.experimental import pallas as pl
from jax.experimental.pallas import tpu as pltpu
from jax.sharding import Mesh, PartitionSpec as P

MOMENT = 0.9
LEARN = 0.5
SHARD = ("yh", "z", "core")
PIECES = (128, 128)
PAIRS = ((0, 0), (0, 1), (1, 0), (1, 1))
F32, BF16 = jnp.float32, jnp.bfloat16
VMEM = 48 * 1024 * 1024
ANY = pl.BlockSpec(memory_space=pl.ANY)


def params(**kw):
    return pltpu.CompilerParams(vmem_limit_bytes=VMEM, **kw)


def cost(flops, bytes_):
    return pl.CostEstimate(flops=flops, bytes_accessed=bytes_, transcendentals=0)


def pack(tokens, biased, weight, place, nz, feats):
    rows = tokens.shape[0]
    kv = biased.shape[-1]
    steps = 4
    zs = nz // steps
    n = len(PIECES)
    half = tokens.shape[1] // 2

    def kernel(place_ref, weight_ref, near, far, numer, current, *outs):
        c = place_ref[1]
        current[...] = (numer[0] / weight_ref[0]).astype(BF16)
        for p, (dy, dc) in enumerate(PAIRS):
            src = far if dy else near
            col = c if dc == 0 else 1 - c
            for z in range(zs):
                start = pl.multiple_of((z * 2 + col) * feats, feats)
                turned = src[:, pl.ds(start, feats)].T
                at = 0
                for k, f in enumerate(PIECES):
                    outs[p * n + k][z * f : (z + 1) * f, :] = turned[at : at + f, :]
                    at += f

    cols = half // steps
    grid = pltpu.PrefetchScalarGridSpec(
        num_scalar_prefetch=1,
        grid=(steps,),
        in_specs=[
            pl.BlockSpec(memory_space=pltpu.SMEM),
            pl.BlockSpec((rows, cols), lambda g, place: (0, place[0] * steps + g)),
            pl.BlockSpec((rows, cols), lambda g, place: (0, (1 - place[0]) * steps + g)),
            pl.BlockSpec((1, feats // steps, kv), lambda g, place: (0, g, 0)),
        ],
        out_specs=[pl.BlockSpec((feats // steps, kv), lambda g, place: (g, 0))]
        + [pl.BlockSpec((zs * f, rows), lambda g, place: (g, 0)) for _ in PAIRS for f in PIECES],
    )
    res = pl.pallas_call(
        kernel,
        grid_spec=grid,
        out_shape=[jax.ShapeDtypeStruct((feats, kv), BF16)]
        + [jax.ShapeDtypeStruct((nz * f, rows), BF16) for _ in PAIRS for f in PIECES],
        compiler_params=params(),
        cost_estimate=cost(0, 6 << 20),
        name="pack",
    )(place, weight, tokens, tokens, biased)
    return res[0], [res[1 + p * n : 1 + (p + 1) * n] for p in range(4)]


def grad_part(xs, cots, nz, extra):
    depth, rows = xs[0].shape
    kv = cots[0].shape[1]

    def kernel(*refs):
        x, c, out = refs[:4], refs[4:8], refs[-1]
        cc = [jnp.concatenate([c[i][...], c[i + 1][...]], axis=0) for i in (0, 2)]
        f = depth // nz
        for z in range(nz):
            s = slice(z * f, (z + 1) * f)
            total = jnp.dot(jnp.concatenate([x[0][s, :], x[1][s, :]], axis=1), cc[0], preferred_element_type=F32)
            total += jnp.dot(jnp.concatenate([x[2][s, :], x[3][s, :]], axis=1), cc[1], preferred_element_type=F32)
            out[z] = total.astype(BF16)

    return pl.pallas_call(
        kernel,
        in_specs=[pl.BlockSpec(memory_space=pltpu.VMEM)] * 8 + [ANY] * len(extra),
        out_specs=pl.BlockSpec(memory_space=pltpu.VMEM),
        out_shape=jax.ShapeDtypeStruct((nz, depth // nz, kv), BF16),
        compiler_params=params(),
        cost_estimate=cost(2 * 4 * depth * rows * kv, 3 << 20),
        name="grad_part",
    )(*xs, *cots, *extra)


def out_part(xs, z_rows, nz, extra):
    n = len(PIECES)
    rows = xs[0][0].shape[1]
    kv = z_rows.shape[1]
    feats = z_rows.shape[0] // nz

    def kernel(*refs):
        x = [refs[p * n : (p + 1) * n] for p in range(4)]
        w = refs[4 * n]
        outs = refs[-4:]
        for p in range(4):
            parts = []
            for z in range(nz):
                for k, f in enumerate(PIECES):
                    parts.append(x[p][k][z * f : (z + 1) * f, :])
            turned = jnp.concatenate(parts, axis=0).T
            total = jnp.dot(turned, w[...], preferred_element_type=F32)
            outs[p][...] = total.astype(outs[p].dtype)

    return pl.pallas_call(
        kernel,
        in_specs=[pl.BlockSpec(memory_space=pltpu.VMEM)] * (4 * n + 1) + [ANY] * len(extra),
        out_specs=[pl.BlockSpec(memory_space=pltpu.VMEM)] * 4,
        out_shape=[jax.ShapeDtypeStruct((rows, kv), F32 if p == 0 else BF16) for p in range(4)],
        compiler_params=params(),
        cost_estimate=cost(2 * 4 * feats * nz * rows * kv, 5 << 20),
        name="out_part",
    )(*[a for part in xs for a in part], z_rows, *extra)


def step(got, biased, momentum, rep_tokens, at, extra):
    nz, f, kv = got.shape

    def kernel(got_ref, numer, moment, *refs):
        velocity, stepped, pushed = refs[-3:]
        g = got_ref[0].astype(F32)
        for z in range(1, nz):
            g += got_ref[z].astype(F32)
        g = g * (1.0 / rep_tokens)
        v = MOMENT * moment[0] + g
        velocity[...] = v
        s = numer[0] - LEARN * (g + MOMENT * v)
        stepped[...] = s
        pushed[...] = s.astype(BF16)

    row = pl.BlockSpec((1, f, kv), lambda i: (0, at // f, 0))
    return pl.pallas_call(
        kernel,
        grid=(1,),
        in_specs=[pl.BlockSpec((nz, f, kv), lambda i: (0, 0, 0)), row, row] + [ANY] * len(extra),
        out_specs=[pl.BlockSpec((f, kv), lambda i: (0, 0))] * 3,
        out_shape=[jax.ShapeDtypeStruct((f, kv), t) for t in (F32, F32, BF16)],
        compiler_params=params(),
        cost_estimate=cost(nz * f * kv, nz * f * kv * 2),
        name="step",
    )(got, biased, momentum, *extra)


def send_push(dist, blocks):
    n = lax.axis_size("replica")
    route = [((i - dist) % n, i) for i in range(n)]
    return [lax.ppermute(b, "replica", route) for b in blocks]


def shards(tokens, cotangent, biased, momentum, weight, round_index):
    hops = lax.axis_size("replica").bit_length() - 1
    power = round_index[0] % hops
    ny, nz, nc = (lax.axis_size(a) for a in SHARD)
    rows, width = tokens.shape
    feats = width // (ny * nz * nc)
    rep_tokens = rows * ny * nz * nc
    place = jnp.stack([lax.axis_index("yh"), lax.axis_index("core")]).astype(jnp.int32)

    def swap(block, pair):
        if pair == (0, 0):
            return block
        plane = [(y, c) for y in range(ny) for c in range(nc)]
        route = [(y * nc + c, (y ^ pair[0]) * nc + (c ^ pair[1])) for y, c in plane]
        return lax.ppermute(block, ("yh", "core"), route)

    cots = [swap(cotangent, pair) for pair in PAIRS]
    current, sent = pack(tokens, biased, weight, place, nz, feats)
    z_rows = lax.all_gather(current, "z", axis=0, tiled=True)
    local = [[swap(b, pair) for b in part] for part, pair in zip(sent, PAIRS)]

    parts = []
    for k in range(len(PIECES)):
        extra = [z_rows] if k == len(PIECES) - 1 else []
        part = grad_part([local[p][k] for p in range(4)], cots, nz, extra)
        parts.append(lax.all_to_all(part, "z", 0, 0, tiled=True))

    mine, *others = out_part(local, z_rows, nz, [])
    others = [swap(o, pair) for o, pair in zip(others, PAIRS[1:])]
    output = (mine + sum(o.astype(F32) for o in others)).astype(BF16)

    branches = [partial(send_push, 1 << level) for level in range(hops)]
    velocity, stepped, arrived = [], [], []
    at = 0
    weight_from = None
    for k, f in enumerate(PIECES):
        v, s, pushed = step(parts[k], biased, momentum, rep_tokens, at, [])
        if k == 0:
            came, weight_from = lax.switch(power, branches, (pushed, weight))
        else:
            (came,) = lax.switch(power, branches, (pushed,))
        velocity.append(v)
        stepped.append(s)
        arrived.append(came)
        at += f
    velocity, stepped, arrived = (jnp.concatenate(a, axis=0) for a in (velocity, stepped, arrived))
    mixed = 0.5 * (stepped + arrived.astype(F32))
    weight_out = 0.5 * (weight + weight_from)
    debiased = mixed / weight_out[0]
    return (output, mixed[None], weight_out, velocity[None], debiased[None])


def solution(mesh):
    n_rep, n_shard = mesh.devices.shape
    inner = Mesh(mesh.devices.reshape(n_rep, 2, n_shard // 4, 2), ("replica",) + SHARD)
    rows = P(("replica",) + SHARD, None)
    held = P("replica", SHARD, None)
    return jax.shard_map(
        shards,
        mesh=inner,
        in_specs=(rows, rows, held, held, P("replica"), P()),
        out_specs=(rows, held, P("replica"), held, held),
        check_vma=False,
    )
```

```python
from functools import partial

import jax
import jax.numpy as jnp
from jax import lax
from jax.experimental import pallas as pl
from jax.experimental.pallas import tpu as pltpu
from jax.sharding import Mesh, PartitionSpec as P

MOMENT = 0.9
LEARN = 0.5
SHARD = ("yh", "z", "core")
F32, BF16 = jnp.float32, jnp.bfloat16
VMEM = pl.BlockSpec(memory_space=pltpu.VMEM)
SMEM = pl.BlockSpec(memory_space=pltpu.SMEM)
ANY = pl.BlockSpec(memory_space=pl.ANY)
TURN = (((0,), (0,)), ((), ()))
TAIL = 16
WAIT = 50_000_000_000


def call(name, kernel, outs, ins, specs, flops=0, moved=0, **kw):
    return pl.pallas_call(
        kernel,
        in_specs=specs,
        out_specs=[VMEM] * len(outs),
        out_shape=[jax.ShapeDtypeStruct(s, t) for s, t in outs],
        compiler_params=pltpu.CompilerParams(vmem_limit_bytes=12 << 20),
        cost_estimate=pl.CostEstimate(flops=flops, bytes_accessed=moved, transcendentals=0),
        name=name,
        **kw,
    )(*ins)


def rounded_rows(biased, weight):
    def kernel(weight_ref, numer, current):
        current[...] = (numer[0] / weight_ref[0]).astype(BF16)

    _, n, kv = biased.shape
    return call("rounded_rows", kernel, [((n, kv), BF16)], (weight, biased), [SMEM, VMEM], moved=n * kv * 6)[0]


def pack(tokens, ny, nz):
    rows, width = tokens.shape
    steps = 4
    zs = nz // steps
    cols = width // ny // steps
    part = width // ny // nz

    def kernel(*refs):
        out = refs[-1]
        for p in range(zs):
            for y in range(ny):
                out[p, :, y * part : (y + 1) * part] = refs[y][:, p * part : (p + 1) * part]

    return pl.pallas_call(
        kernel,
        grid=(steps,),
        in_specs=[pl.BlockSpec((rows, cols), lambda g, y=y: (0, y * steps + g)) for y in range(ny)],
        out_specs=pl.BlockSpec((zs, rows, ny * part), lambda g: (g, 0, 0)),
        out_shape=jax.ShapeDtypeStruct((nz, rows, ny * part), BF16),
        compiler_params=pltpu.CompilerParams(vmem_limit_bytes=60 << 20),
        cost_estimate=pl.CostEstimate(flops=0, bytes_accessed=4 * rows * width, transcendentals=0),
        name="pack",
    )(*[tokens] * ny)


def join(first, second):
    n, kv = first.shape

    def kernel(first_ref, second_ref, out):
        out[:n] = first_ref[...]
        out[n:] = second_ref[...]

    return call("join", kernel, [((2 * n, kv), BF16)], (first, second), [VMEM] * 2, flops=WAIT)[0]


def columns(place_ref, dy, dc, feats):
    y = 1 - place_ref[0] if dy else place_ref[0]
    c = 1 - place_ref[1] if dc else place_ref[1]
    return pl.ds(pl.multiple_of((y * 2 + c) * feats, feats), feats)


def out_part(x, near, far, place):
    nz, n, _ = x.shape
    depth, kv = near.shape

    def kernel(place_ref, x_ref, near_ref, far_ref, out):
        y = place_ref[0]
        own = pl.ds(pl.multiple_of(y * depth, depth), depth)
        other = pl.ds(pl.multiple_of((1 - y) * depth, depth), depth)
        for z in range(0, nz, 2):
            total = jnp.zeros((2 * n, kv), F32)
            for cols, w_ref in ((own, near_ref), (other, far_ref)):
                block = jnp.concatenate([x_ref[z, :, cols], x_ref[z + 1, :, cols]], axis=0)
                total += jnp.dot(block, w_ref[...], preferred_element_type=F32)
            out[z] = total[:n].astype(BF16)
            out[z + 1] = total[n:].astype(BF16)

    return call(
        "out_part",
        kernel,
        [((nz, n, kv), BF16)],
        (place, x, near, far),
        [SMEM] + [VMEM] * 3,
        flops=WAIT,
        moved=4 << 20,
    )[0]


def grad_block(place_ref, x_ref, c_refs, turns, dy, dc, feats):
    cols = columns(place_ref, dy, dc, feats)
    nz = x_ref.shape[0]
    total = jnp.zeros((feats, c_refs[0].shape[-1]), F32)
    for c_ref, group in zip(c_refs, turns):
        blocks = [x_ref[lax.rem(place_ref[2] - t + nz, nz), :, cols] for t in group]
        block = blocks[0] if len(blocks) == 1 else jnp.concatenate(blocks, axis=0)
        total += lax.dot_general(block, c_ref[...], TURN, preferred_element_type=F32)
    return total


def grad_sent(x, cots, turns, place, feats):
    kv = cots[0].shape[1]

    def kernel(place_ref, x_ref, *refs):
        for dy in (0, 1):
            refs[-1][dy] = grad_block(place_ref, x_ref, refs[:-1], turns, dy, 1, feats).astype(BF16)

    return call(
        "grad_sent",
        kernel,
        [((2, feats, kv), BF16)],
        (place, x, *cots),
        [SMEM, VMEM] + [VMEM] * len(cots),
        flops=2 * WAIT,
        moved=3 << 20,
    )[0]


def grad_kept(x, cots, turns, place, feats):
    kv = cots[0].shape[1]

    def kernel(place_ref, x_ref, *refs):
        for dy in (0, 1):
            refs[-1][dy] = grad_block(place_ref, x_ref, refs[:-1], turns, dy, 0, feats)

    return call(
        "grad_kept",
        kernel,
        [((2, feats, kv), F32)],
        (place, x, *cots),
        [SMEM, VMEM] + [VMEM] * len(cots),
        flops=4 * x.shape[0] * x.shape[1] * feats * kv,
        moved=3 << 20,
    )[0]


def grad_far(kept, given):
    def kernel(kept_ref, given_ref, out):
        out[...] = (kept_ref[1] + given_ref[1].astype(F32)).astype(BF16)

    return call("grad_far", kernel, [(kept.shape[1:], BF16)], (kept, given), [VMEM] * 2, flops=kept.size)[0]


def step(kept, given, got, biased, momentum, weight, rep_tokens):
    size, kv = got.shape

    def kernel(w_ref, kept_ref, given_ref, got_ref, numer, moment, velocity, stepped, pushed):
        g = kept_ref[0] + given_ref[0].astype(F32) + got_ref[...].astype(F32)
        g = g * (1.0 / rep_tokens)
        v = MOMENT * moment[0] + g
        velocity[0] = v
        s = numer[0] - LEARN * (g + MOMENT * v)
        stepped[...] = s
        pushed[:size] = s.astype(BF16)
        whole = jnp.full((TAIL, kv), w_ref[0], F32)
        high = whole.astype(BF16).astype(F32)
        middle = (whole - high).astype(BF16).astype(F32)
        low = whole - high - middle
        row = lax.broadcasted_iota(jnp.int32, (TAIL, kv), 0)
        pushed[size:] = jnp.where(row == 0, high, jnp.where(row == 1, middle, low)).astype(BF16)

    return call(
        "step",
        kernel,
        [((1, size, kv), F32), ((size, kv), F32), ((size + TAIL, kv), BF16)],
        (weight, kept, given, got, biased, momentum),
        [SMEM] + [VMEM] * 5,
        flops=8 * size * kv,
        moved=24 * size * kv,
    )


def mix(stepped, arrived, weight, after):
    size, kv = stepped.shape

    def kernel(w_ref, _, s, a, weight_out, mixed_out, debiased_out):
        parts = a[size:].astype(F32)
        w = 0.5 * (w_ref[0] + (parts[0:1] + parts[1:2] + parts[2:3]))
        weight_out[0] = w[0, 0]
        mixed = 0.5 * (s[...] + a[:size].astype(F32))
        mixed_out[0] = mixed
        debiased_out[0] = mixed / w

    full = jax.ShapeDtypeStruct((1, size, kv), F32)
    return pl.pallas_call(
        kernel,
        in_specs=[SMEM, ANY] + [VMEM] * 2,
        out_specs=[SMEM] + [VMEM] * 2,
        out_shape=[jax.ShapeDtypeStruct((1,), F32)] + [full] * 2,
        compiler_params=pltpu.CompilerParams(vmem_limit_bytes=12 << 20),
        cost_estimate=pl.CostEstimate(flops=6 * size * kv, bytes_accessed=22 * size * kv, transcendentals=0),
        name="mix",
    )(weight, after, stepped, arrived)


def sum_parts(parts):
    nz, rows, kv = parts.shape

    def kernel(parts_ref, out):
        total = parts_ref[0].astype(F32)
        for z in range(1, nz):
            total += parts_ref[z].astype(F32)
        out[...] = total.astype(BF16)

    return call("sum_parts", kernel, [((rows, kv), BF16)], (parts,), [VMEM], flops=parts.size, moved=2 * parts.size)[0]


def push_round(dist, tokens, cotangent, biased, momentum, weight):
    ny, nz, nc = (lax.axis_size(a) for a in SHARD)
    rows, width = tokens.shape
    feats = width // (ny * nz * nc)
    rep_tokens = rows * ny * nz * nc
    swap = ((0, 1), (1, 0))
    n_rep = lax.axis_size("replica")
    ahead = [((i - dist) % n_rep, i) for i in range(n_rep)]
    place = jnp.stack([lax.axis_index(a) for a in ("yh", "core", "z")]).astype(jnp.int32)

    def along(block, turn):
        return lax.ppermute(block, "z", [(i, (i + turn) % nz) for i in range(nz)])

    pair = join(cotangent, along(cotangent, 4))
    x = lax.all_to_all(pack(tokens, ny, nz), "z", 0, 0, tiled=True)
    cots = [pair, along(cotangent, 2), along(cotangent, -2), along(pair, 1), along(pair, -1)]
    turns = [(0, 4), (2,), (6,), (1, 5), (7, 3)]

    near = lax.all_gather(rounded_rows(biased, weight), "core", axis=0, tiled=True)
    far = lax.ppermute(near, "yh", swap)
    part = out_part(x, near, far, place)
    parts = lax.all_to_all(part, "z", 0, 0, tiled=True)

    given = lax.ppermute(grad_sent(x, cots, turns, place, feats), "core", swap)
    kept = grad_kept(x, cots, turns, place, feats)
    got = lax.ppermute(grad_far(kept, given), "yh", swap)
    output = sum_parts(parts)

    velocity, stepped, pushed = step(kept, given, got, biased, momentum, weight, rep_tokens)
    arrived = lax.ppermute(pushed, "replica", ahead)
    weight_out, mixed, debiased = mix(stepped, arrived, weight, output)
    return output, mixed, weight_out, velocity, debiased


def shards(tokens, cotangent, biased, momentum, weight, round_index):
    hops = lax.axis_size("replica").bit_length() - 1
    power = round_index[0] % hops
    branches = [partial(push_round, 1 << level) for level in range(hops)]
    return lax.switch(power, branches, tokens, cotangent, biased, momentum, weight)


def solution(mesh):
    n_rep, n_shard = mesh.devices.shape
    inner = Mesh(mesh.devices.reshape(n_rep, 2, n_shard // 4, 2), ("replica",) + SHARD)
    rows = P(("replica",) + SHARD, None)
    held = P("replica", SHARD, None)
    return jax.shard_map(
        shards,
        mesh=inner,
        in_specs=(rows, rows, held, held, P("replica"), P()),
        out_specs=(rows, held, P("replica"), held, held),
        check_vma=False,
    )
```

```python
from functools import partial

import jax
import jax.numpy as jnp
from jax import lax
from jax.experimental import pallas as pl
from jax.experimental.pallas import tpu as pltpu
from jax.sharding import Mesh, PartitionSpec as P

MOMENT = 0.9
LEARN = 0.5
SHARD = ("yh", "z", "core")
F32, BF16 = jnp.float32, jnp.bfloat16
VMEM = pl.BlockSpec(memory_space=pltpu.VMEM)
SMEM = pl.BlockSpec(memory_space=pltpu.SMEM)
ANY = pl.BlockSpec(memory_space=pl.ANY)
TURN = (((0,), (0,)), ((), ()))
TAIL = 16
WAIT = 50_000_000_000


def call(name, kernel, outs, ins, specs, flops=0, moved=0, **kw):
    return pl.pallas_call(
        kernel,
        in_specs=specs,
        out_specs=[VMEM] * len(outs),
        out_shape=[jax.ShapeDtypeStruct(s, t) for s, t in outs],
        compiler_params=pltpu.CompilerParams(vmem_limit_bytes=12 << 20),
        cost_estimate=pl.CostEstimate(flops=flops, bytes_accessed=moved, transcendentals=0),
        name=name,
        **kw,
    )(*ins)


def rounded_rows(biased, weight, after):
    def kernel(weight_ref, _, numer, current):
        current[...] = (numer[0] / weight_ref[0]).astype(BF16)

    _, n, kv = biased.shape
    return call("rounded_rows", kernel, [((n, kv), BF16)], (weight, after, biased), [SMEM, ANY, VMEM])[0]


def pack(tokens, cotangent, ny, nz):
    rows, width = tokens.shape
    kv = cotangent.shape[1]
    steps = 2
    zs = nz // steps
    cols = width // ny // steps
    part = width // ny // nz

    def kernel(cot, *refs):
        out, kept = refs[-2:]
        kept[...] = cot[...]
        for p in range(zs):
            for y in range(ny):
                out[p, :, y * part : (y + 1) * part] = refs[y][:, p * part : (p + 1) * part]

    return pl.pallas_call(
        kernel,
        grid=(steps,),
        in_specs=[pl.BlockSpec((rows // steps, kv), lambda g: (g, 0))]
        + [pl.BlockSpec((rows, cols), lambda g, y=y: (0, y * steps + g)) for y in range(ny)],
        out_specs=[
            pl.BlockSpec((zs, rows, ny * part), lambda g: (g, 0, 0)),
            pl.BlockSpec((rows // steps, kv), lambda g: (g, 0)),
        ],
        out_shape=[
            jax.ShapeDtypeStruct((nz, rows, ny * part), BF16),
            jax.ShapeDtypeStruct((rows, kv), BF16),
        ],
        compiler_params=pltpu.CompilerParams(vmem_limit_bytes=60 << 20),
        cost_estimate=pl.CostEstimate(flops=0, bytes_accessed=4 * rows * width, transcendentals=0),
        name="pack",
    )(cotangent, *[tokens] * ny)


def join(first, second):
    n, kv = first.shape

    def kernel(first_ref, second_ref, out, alone):
        out[:n] = first_ref[...]
        out[n:] = second_ref[...]
        alone[...] = first_ref[...]

    outs = [((2 * n, kv), BF16), ((n, kv), BF16)]
    return call("join", kernel, outs, (first, second), [VMEM] * 2, flops=WAIT)


def columns(place_ref, dy, dc, feats):
    y = 1 - place_ref[0] if dy else place_ref[0]
    c = 1 - place_ref[1] if dc else place_ref[1]
    return pl.ds(pl.multiple_of((y * 2 + c) * feats, feats), feats)


def out_part(x, near, far, place):
    nz, n, _ = x.shape
    depth, kv = near.shape
    steps = 2
    zs = nz // steps

    def kernel(place_ref, x_ref, near_ref, far_ref, out):
        y = place_ref[0]
        own = pl.ds(pl.multiple_of(y * depth, depth), depth)
        other = pl.ds(pl.multiple_of((1 - y) * depth, depth), depth)
        base = pl.program_id(0) * zs
        for z in range(0, zs, 2):
            total = jnp.zeros((2 * n, kv), F32)
            for cols, w_ref in ((own, near_ref), (other, far_ref)):
                block = jnp.concatenate([x_ref[base + z, :, cols], x_ref[base + z + 1, :, cols]], axis=0)
                total += jnp.dot(block, w_ref[...], preferred_element_type=F32)
            out[z] = total[:n].astype(BF16)
            out[z + 1] = total[n:].astype(BF16)

    return pl.pallas_call(
        kernel,
        grid=(steps,),
        in_specs=[SMEM] + [VMEM] * 3,
        out_specs=pl.BlockSpec((zs, n, kv), lambda g: (g, 0, 0)),
        out_shape=jax.ShapeDtypeStruct((nz, n, kv), BF16),
        compiler_params=pltpu.CompilerParams(vmem_limit_bytes=12 << 20),
        cost_estimate=pl.CostEstimate(flops=WAIT, bytes_accessed=4 << 20, transcendentals=0),
        name="out_part",
    )(place, x, near, far)


def grad_block(place_ref, x_ref, c_refs, turns, dy, dc, feats):
    cols = columns(place_ref, dy, dc, feats)
    nz = x_ref.shape[0]
    total = None
    at = 0
    for group in turns:
        refs, at = c_refs[at : at + len(group)], at + len(group)
        blocks = [x_ref[lax.rem(place_ref[2] - t + nz, nz), :, cols] for pair in group for t in pair]
        cots = refs[0][...] if len(refs) == 1 else jnp.concatenate([r[...] for r in refs], axis=0)
        part = lax.dot_general(jnp.concatenate(blocks, axis=0), cots, TURN, preferred_element_type=F32)
        total = part if total is None else total + part
    return total


def grad_part(name, x, cots, turns, place, feats, which, start, out_type, hint, after):
    kv = cots[0].shape[1]
    more = [] if start is None else [start]

    def kernel(place_ref, x_ref, *refs):
        out = refs[-1]
        for i, (dy, dc) in enumerate(which):
            total = grad_block(place_ref, x_ref, refs[: len(cots)], turns, dy, dc, feats)
            if more:
                total += refs[len(cots)][dc * 2 + dy]
            out[i] = total.astype(out_type)

    return call(
        name,
        kernel,
        [((len(which), feats, kv), out_type)],
        (place, x, *cots, *more, *after),
        [SMEM, VMEM] + [VMEM] * (len(cots) + len(more)) + [ANY] * len(after),
        flops=hint,
        moved=3 << 20,
    )[0]


def grad_far(kept, given):
    def kernel(kept_ref, given_ref, out):
        out[...] = (kept_ref[1] + given_ref[1].astype(F32)).astype(BF16)

    return call("grad_far", kernel, [(kept.shape[1:], BF16)], (kept, given), [VMEM] * 2, flops=kept.size)[0]


def step(kept, given, got, biased, momentum, weight, rep_tokens):
    size, kv = got.shape

    def kernel(w_ref, kept_ref, given_ref, got_ref, numer, moment, velocity, stepped, pushed):
        g = kept_ref[0] + given_ref[0].astype(F32) + got_ref[...].astype(F32)
        g = g * (1.0 / rep_tokens)
        v = MOMENT * moment[0] + g
        velocity[0] = v
        s = numer[0] - LEARN * (g + MOMENT * v)
        stepped[...] = s
        pushed[:size] = s.astype(BF16)
        whole = jnp.full((TAIL, kv), w_ref[0], F32)
        high = whole.astype(BF16).astype(F32)
        middle = (whole - high).astype(BF16).astype(F32)
        low = whole - high - middle
        row = lax.broadcasted_iota(jnp.int32, (TAIL, kv), 0)
        pushed[size:] = jnp.where(row == 0, high, jnp.where(row == 1, middle, low)).astype(BF16)

    return call(
        "step",
        kernel,
        [((1, size, kv), F32), ((size, kv), F32), ((size + TAIL, kv), BF16)],
        (weight, kept, given, got, biased, momentum),
        [SMEM] + [VMEM] * 5,
        flops=8 * size * kv,
        moved=24 * size * kv,
    )


def mix(stepped, arrived, weight, after):
    size, kv = stepped.shape
    steps = 2

    def kernel(w_ref, _, s, a, tail, weight_out, mixed_out, debiased_out):
        parts = tail[...].astype(F32)
        w = 0.5 * (w_ref[0] + (parts[0:1] + parts[1:2] + parts[2:3]))
        weight_out[0] = w[0, 0]
        mixed = 0.5 * (s[...] + a[...].astype(F32))
        mixed_out[0] = mixed
        debiased_out[0] = mixed / w

    full = jax.ShapeDtypeStruct((1, size, kv), F32)
    piece = pl.BlockSpec((size // steps, kv), lambda g: (g, 0))
    piece_out = pl.BlockSpec((1, size // steps, kv), lambda g: (0, g, 0))
    return pl.pallas_call(
        kernel,
        grid=(steps,),
        in_specs=[SMEM, ANY, piece, piece, pl.BlockSpec((TAIL, kv), lambda g: (size // TAIL, 0))],
        out_specs=[SMEM, piece_out, piece_out],
        out_shape=[jax.ShapeDtypeStruct((1,), F32)] + [full] * 2,
        compiler_params=pltpu.CompilerParams(vmem_limit_bytes=12 << 20),
        cost_estimate=pl.CostEstimate(flops=6 * size * kv, bytes_accessed=22 * size * kv, transcendentals=0),
        name="mix",
    )(weight, after, stepped, arrived, arrived)


def sum_parts(parts):
    nz, rows, kv = parts.shape

    def kernel(parts_ref, out):
        total = parts_ref[0].astype(F32)
        for z in range(1, nz):
            total += parts_ref[z].astype(F32)
        out[...] = total.astype(BF16)

    return call("sum_parts", kernel, [((rows, kv), BF16)], (parts,), [VMEM], flops=parts.size, moved=2 * parts.size)[0]


def push_round(dist, packed, own, biased, momentum, weight):
    ny, nz, nc = (lax.axis_size(a) for a in SHARD)
    feats = biased.shape[1]
    rep_tokens = own.shape[0] * ny * nz * nc
    swap = ((0, 1), (1, 0))
    n_rep = lax.axis_size("replica")
    ahead = [((i - dist) % n_rep, i) for i in range(n_rep)]
    place = jnp.stack([lax.axis_index(a) for a in ("yh", "core", "z")]).astype(jnp.int32)

    def along(block, turn):
        return lax.ppermute(block, "z", [(i, (i + turn) % nz) for i in range(nz)])

    pair, alone = join(own, along(own, 4))
    x = lax.all_to_all(packed, "z", 0, 0, tiled=True)
    first = [pair, along(alone, 2), along(alone, -2)]
    first_turns = [((0, 4),), ((2,), (6,))]
    last = [along(pair, 1), along(pair, -1)]
    last_turns = [((1, 5),), ((7, 3),)]

    near = lax.all_gather(rounded_rows(biased, weight, alone), "core", axis=0, tiled=True)
    far = lax.ppermute(near, "yh", swap)
    part = out_part(x, near, far, place)
    parts = lax.all_to_all(part, "z", 0, 0, tiled=True)

    mine, other = ((0, 0), (1, 0)), ((0, 1), (1, 1))
    start = grad_part("grad_first", x, first, first_turns, place, feats, mine + other, None, F32, WAIT, [part])
    given = grad_part("grad_sent", x, last, last_turns, place, feats, other, start, BF16, 2 * WAIT, [])
    given = lax.ppermute(given, "core", swap)
    kept = grad_part("grad_kept", x, last, last_turns, place, feats, mine, start, F32, 0, [])
    got = lax.ppermute(grad_far(kept, given), "yh", swap)
    output = sum_parts(parts)

    velocity, stepped, pushed = step(kept, given, got, biased, momentum, weight, rep_tokens)
    arrived = lax.ppermute(pushed, "replica", ahead)
    weight_out, mixed, debiased = mix(stepped, arrived, weight, output)
    return output, mixed, weight_out, velocity, debiased


def shards(tokens, cotangent, biased, momentum, weight, round_index):
    hops = lax.axis_size("replica").bit_length() - 1
    power = round_index[0] % hops
    branches = [partial(push_round, 1 << level) for level in range(hops)]
    packed, own = pack(tokens, cotangent, lax.axis_size("yh"), lax.axis_size("z"))
    return lax.switch(power, branches, packed, own, biased, momentum, weight)


def solution(mesh):
    n_rep, n_shard = mesh.devices.shape
    inner = Mesh(mesh.devices.reshape(n_rep, 2, n_shard // 4, 2), ("replica",) + SHARD)
    rows = P(("replica",) + SHARD, None)
    held = P("replica", SHARD, None)
    return jax.shard_map(
        shards,
        mesh=inner,
        in_specs=(rows, rows, held, held, P("replica"), P()),
        out_specs=(rows, held, P("replica"), held, held),
        check_vma=False,
    )
```

```python
from functools import partial

import jax
import jax.numpy as jnp
from jax import lax
from jax.experimental import pallas as pl
from jax.experimental.pallas import tpu as pltpu
from jax.sharding import Mesh, PartitionSpec as P

MOMENT = 0.9
LEARN = 0.5
SHARD = ("yh", "z", "core")
F32, BF16 = jnp.float32, jnp.bfloat16
VMEM = pl.BlockSpec(memory_space=pltpu.VMEM)
SMEM = pl.BlockSpec(memory_space=pltpu.SMEM)
ANY = pl.BlockSpec(memory_space=pl.ANY)
TURN = (((0,), (0,)), ((), ()))
TAIL = 16
WAIT = 50_000_000_000


def call(name, kernel, outs, ins, specs, flops=0, moved=0, **kw):
    return pl.pallas_call(
        kernel,
        in_specs=specs,
        out_specs=[VMEM] * len(outs),
        out_shape=[jax.ShapeDtypeStruct(s, t) for s, t in outs],
        compiler_params=pltpu.CompilerParams(vmem_limit_bytes=12 << 20),
        cost_estimate=pl.CostEstimate(flops=flops, bytes_accessed=moved, transcendentals=0),
        name=name,
        **kw,
    )(*ins)


def rounded_rows(biased, weight, after):
    def kernel(weight_ref, _, numer, current):
        current[...] = (numer[0] / weight_ref[0]).astype(BF16)

    _, n, kv = biased.shape
    return call("rounded_rows", kernel, [((n, kv), BF16)], (weight, after, biased), [SMEM, ANY, VMEM])[0]


def pack(tokens, ny, nz):
    rows, width = tokens.shape
    steps = 2
    zs = nz // steps
    cols = width // ny // steps
    part = width // ny // nz

    def kernel(*refs):
        out = refs[-1]
        for p in range(zs):
            for y in range(ny):
                out[p, :, y * part : (y + 1) * part] = refs[y][:, p * part : (p + 1) * part]

    return pl.pallas_call(
        kernel,
        grid=(steps,),
        in_specs=[pl.BlockSpec((rows, cols), lambda g, y=y: (0, y * steps + g)) for y in range(ny)],
        out_specs=pl.BlockSpec((zs, rows, ny * part), lambda g: (g, 0, 0)),
        out_shape=jax.ShapeDtypeStruct((nz, rows, ny * part), BF16),
        compiler_params=pltpu.CompilerParams(vmem_limit_bytes=60 << 20),
        cost_estimate=pl.CostEstimate(flops=0, bytes_accessed=4 * rows * width, transcendentals=0),
        name="pack",
    )(*[tokens] * ny)


def join(first, second):
    n, kv = first.shape

    def kernel(first_ref, second_ref, out, alone):
        out[:n] = first_ref[...]
        out[n:] = second_ref[...]
        alone[...] = first_ref[...]

    outs = [((2 * n, kv), BF16), ((n, kv), BF16)]
    return call("join", kernel, outs, (first, second), [VMEM] * 2, flops=WAIT)


def columns(place_ref, dy, dc, feats):
    y = 1 - place_ref[0] if dy else place_ref[0]
    c = 1 - place_ref[1] if dc else place_ref[1]
    return pl.ds(pl.multiple_of((y * 2 + c) * feats, feats), feats)


def out_part(x, near, far, place):
    nz, n, _ = x.shape
    depth, kv = near.shape
    steps = 2
    zs = nz // steps

    def kernel(place_ref, x_ref, near_ref, far_ref, out):
        y = place_ref[0]
        own = pl.ds(pl.multiple_of(y * depth, depth), depth)
        other = pl.ds(pl.multiple_of((1 - y) * depth, depth), depth)
        base = pl.program_id(0) * zs
        for z in range(0, zs, 2):
            total = jnp.zeros((2 * n, kv), F32)
            for cols, w_ref in ((own, near_ref), (other, far_ref)):
                block = jnp.concatenate([x_ref[base + z, :, cols], x_ref[base + z + 1, :, cols]], axis=0)
                total += jnp.dot(block, w_ref[...], preferred_element_type=F32)
            out[z] = total[:n].astype(BF16)
            out[z + 1] = total[n:].astype(BF16)

    return pl.pallas_call(
        kernel,
        grid=(steps,),
        in_specs=[SMEM] + [VMEM] * 3,
        out_specs=pl.BlockSpec((zs, n, kv), lambda g: (g, 0, 0)),
        out_shape=jax.ShapeDtypeStruct((nz, n, kv), BF16),
        compiler_params=pltpu.CompilerParams(vmem_limit_bytes=12 << 20),
        cost_estimate=pl.CostEstimate(flops=WAIT, bytes_accessed=4 << 20, transcendentals=0),
        name="out_part",
    )(place, x, near, far)


def grad_block(place_ref, x_ref, c_refs, turns, dy, dc, feats):
    cols = columns(place_ref, dy, dc, feats)
    nz = x_ref.shape[0]
    total = None
    at = 0
    for group in turns:
        refs, at = c_refs[at : at + len(group)], at + len(group)
        blocks = [x_ref[lax.rem(place_ref[2] - t + nz, nz), :, cols] for pair in group for t in pair]
        cots = refs[0][...] if len(refs) == 1 else jnp.concatenate([r[...] for r in refs], axis=0)
        part = lax.dot_general(jnp.concatenate(blocks, axis=0), cots, TURN, preferred_element_type=F32)
        total = part if total is None else total + part
    return total


def grad_part(name, x, cots, turns, place, feats, which, start, out_type, hint, after):
    kv = cots[0].shape[1]
    more = [] if start is None else [start]

    def kernel(place_ref, x_ref, *refs):
        out = refs[-1]
        for i, (dy, dc) in enumerate(which):
            total = grad_block(place_ref, x_ref, refs[: len(cots)], turns, dy, dc, feats)
            if more:
                total += refs[len(cots)][dc * 2 + dy]
            out[i] = total.astype(out_type)

    return call(
        name,
        kernel,
        [((len(which), feats, kv), out_type)],
        (place, x, *cots, *more, *after),
        [SMEM, VMEM] + [VMEM] * (len(cots) + len(more)) + [ANY] * len(after),
        flops=hint,
        moved=3 << 20,
    )[0]


def grad_far(kept, given):
    def kernel(kept_ref, given_ref, out):
        out[...] = (kept_ref[1] + given_ref[1].astype(F32)).astype(BF16)

    return call("grad_far", kernel, [(kept.shape[1:], BF16)], (kept, given), [VMEM] * 2, flops=kept.size)[0]


def step(kept, given, got, biased, momentum, weight, rep_tokens):
    size, kv = got.shape

    def kernel(w_ref, kept_ref, given_ref, got_ref, numer, moment, velocity, stepped, pushed):
        g = kept_ref[0] + given_ref[0].astype(F32) + got_ref[...].astype(F32)
        g = g * (1.0 / rep_tokens)
        v = MOMENT * moment[0] + g
        velocity[0] = v
        s = numer[0] - LEARN * (g + MOMENT * v)
        stepped[...] = s
        pushed[:size] = s.astype(BF16)
        whole = jnp.full((TAIL, kv), w_ref[0], F32)
        high = whole.astype(BF16).astype(F32)
        middle = (whole - high).astype(BF16).astype(F32)
        low = whole - high - middle
        row = lax.broadcasted_iota(jnp.int32, (TAIL, kv), 0)
        pushed[size:] = jnp.where(row == 0, high, jnp.where(row == 1, middle, low)).astype(BF16)

    return call(
        "step",
        kernel,
        [((1, size, kv), F32), ((size, kv), F32), ((size + TAIL, kv), BF16)],
        (weight, kept, given, got, biased, momentum),
        [SMEM] + [VMEM] * 5,
        flops=8 * size * kv,
        moved=24 * size * kv,
    )


def mix(stepped, arrived, weight, after):
    size, kv = stepped.shape
    steps = 2

    def kernel(w_ref, _, s, a, tail, weight_out, mixed_out, debiased_out):
        parts = tail[...].astype(F32)
        w = 0.5 * (w_ref[0] + (parts[0:1] + parts[1:2] + parts[2:3]))
        weight_out[0] = w[0, 0]
        mixed = 0.5 * (s[...] + a[...].astype(F32))
        mixed_out[0] = mixed
        debiased_out[0] = mixed / w

    full = jax.ShapeDtypeStruct((1, size, kv), F32)
    piece = pl.BlockSpec((size // steps, kv), lambda g: (g, 0))
    piece_out = pl.BlockSpec((1, size // steps, kv), lambda g: (0, g, 0))
    return pl.pallas_call(
        kernel,
        grid=(steps,),
        in_specs=[SMEM, ANY, piece, piece, pl.BlockSpec((TAIL, kv), lambda g: (size // TAIL, 0))],
        out_specs=[SMEM, piece_out, piece_out],
        out_shape=[jax.ShapeDtypeStruct((1,), F32)] + [full] * 2,
        compiler_params=pltpu.CompilerParams(vmem_limit_bytes=12 << 20),
        cost_estimate=pl.CostEstimate(flops=6 * size * kv, bytes_accessed=22 * size * kv, transcendentals=0),
        name="mix",
    )(weight, after, stepped, arrived, arrived)


def sum_parts(parts):
    nz, rows, kv = parts.shape

    def kernel(parts_ref, out):
        total = parts_ref[0].astype(F32)
        for z in range(1, nz):
            total += parts_ref[z].astype(F32)
        out[...] = total.astype(BF16)

    return call("sum_parts", kernel, [((rows, kv), BF16)], (parts,), [VMEM], flops=parts.size, moved=2 * parts.size)[0]


def push_round(dist, tokens, own, biased, momentum, weight):
    ny, nz, nc = (lax.axis_size(a) for a in SHARD)
    feats = biased.shape[1]
    rep_tokens = own.shape[0] * ny * nz * nc
    swap = ((0, 1), (1, 0))
    n_rep = lax.axis_size("replica")
    ahead = [((i - dist) % n_rep, i) for i in range(n_rep)]
    place = jnp.stack([lax.axis_index(a) for a in ("yh", "core", "z")]).astype(jnp.int32)

    def along(block, turn):
        return lax.ppermute(block, "z", [(i, (i + turn) % nz) for i in range(nz)])

    pair, alone = join(own, along(own, 4))
    x = lax.all_to_all(pack(tokens, ny, nz), "z", 0, 0, tiled=True)
    first = [pair, along(alone, 2), along(alone, -2)]
    first_turns = [((0, 4),), ((2,), (6,))]
    last = [along(pair, 1), along(pair, -1)]
    last_turns = [((1, 5),), ((7, 3),)]

    near = lax.all_gather(rounded_rows(biased, weight, alone), "core", axis=0, tiled=True)
    far = lax.ppermute(near, "yh", swap)
    part = out_part(x, near, far, place)
    parts = lax.all_to_all(part, "z", 0, 0, tiled=True)

    mine, other = ((0, 0), (1, 0)), ((0, 1), (1, 1))
    start = grad_part("grad_first", x, first, first_turns, place, feats, mine + other, None, F32, WAIT, [part])
    given = grad_part("grad_sent", x, last, last_turns, place, feats, other, start, BF16, 2 * WAIT, [])
    given = lax.ppermute(given, "core", swap)
    kept = grad_part("grad_kept", x, last, last_turns, place, feats, mine, start, F32, 0, [])
    got = lax.ppermute(grad_far(kept, given), "yh", swap)
    output = sum_parts(parts)

    velocity, stepped, pushed = step(kept, given, got, biased, momentum, weight, rep_tokens)
    arrived = lax.ppermute(pushed, "replica", ahead)
    weight_out, mixed, debiased = mix(stepped, arrived, weight, output)
    return output, mixed, weight_out, velocity, debiased


def shards(tokens, cotangent, biased, momentum, weight, round_index):
    hops = lax.axis_size("replica").bit_length() - 1
    power = round_index[0] % hops
    branches = [partial(push_round, 1 << level) for level in range(hops)]
    return lax.switch(power, branches, tokens, cotangent, biased, momentum, weight)


def solution(mesh):
    n_rep, n_shard = mesh.devices.shape
    inner = Mesh(mesh.devices.reshape(n_rep, 2, n_shard // 4, 2), ("replica",) + SHARD)
    rows = P(("replica",) + SHARD, None)
    held = P("replica", SHARD, None)
    return jax.shard_map(
        shards,
        mesh=inner,
        in_specs=(rows, rows, held, held, P("replica"), P()),
        out_specs=(rows, held, P("replica"), held, held),
        check_vma=False,
    )
```

```python
from functools import partial

import jax
import jax.numpy as jnp
from jax import lax
from jax.experimental import pallas as pl
from jax.experimental.pallas import tpu as pltpu
from jax.sharding import Mesh, PartitionSpec as P

MOMENT = 0.9
LEARN = 0.5
SHARD = ("yh", "z", "core")
F32, BF16 = jnp.float32, jnp.bfloat16
VMEM = pl.BlockSpec(memory_space=pltpu.VMEM)
SMEM = pl.BlockSpec(memory_space=pltpu.SMEM)
ANY = pl.BlockSpec(memory_space=pl.ANY)
TURN = (((0,), (0,)), ((), ()))
TAIL = 16
WAIT = 50_000_000_000


def call(name, kernel, outs, ins, specs, flops=0, moved=0, **kw):
    return pl.pallas_call(
        kernel,
        in_specs=specs,
        out_specs=[VMEM] * len(outs),
        out_shape=[jax.ShapeDtypeStruct(s, t) for s, t in outs],
        compiler_params=pltpu.CompilerParams(vmem_limit_bytes=12 << 20),
        cost_estimate=pl.CostEstimate(flops=flops, bytes_accessed=moved, transcendentals=0),
        name=name,
        **kw,
    )(*ins)


def rounded_rows(biased, weight, after):
    def kernel(weight_ref, _, numer, current):
        current[...] = (numer[0] / weight_ref[0]).astype(BF16)

    _, n, kv = biased.shape
    return call("rounded_rows", kernel, [((n, kv), BF16)], (weight, after, biased), [SMEM, ANY, VMEM])[0]


def pack(tokens, ny, nz):
    rows, width = tokens.shape
    steps = 2
    zs = nz // steps
    cols = width // ny // steps
    part = width // ny // nz

    def kernel(*refs):
        out = refs[-1]
        for p in range(zs):
            for y in range(ny):
                out[p, :, y * part : (y + 1) * part] = refs[y][:, p * part : (p + 1) * part]

    return pl.pallas_call(
        kernel,
        grid=(steps,),
        in_specs=[pl.BlockSpec((rows, cols), lambda g, y=y: (0, y * steps + g)) for y in range(ny)],
        out_specs=pl.BlockSpec((zs, rows, ny * part), lambda g: (g, 0, 0)),
        out_shape=jax.ShapeDtypeStruct((nz, rows, ny * part), BF16),
        compiler_params=pltpu.CompilerParams(vmem_limit_bytes=60 << 20),
        cost_estimate=pl.CostEstimate(flops=0, bytes_accessed=4 * rows * width, transcendentals=0),
        name="pack",
    )(*[tokens] * ny)


def join(first, second):
    n, kv = first.shape

    def kernel(first_ref, second_ref, out, alone):
        out[:n] = first_ref[...]
        out[n:] = second_ref[...]
        alone[...] = first_ref[...]

    outs = [((2 * n, kv), BF16), ((n, kv), BF16)]
    return call("join", kernel, outs, (first, second), [VMEM] * 2, flops=WAIT)


def columns(place_ref, dy, dc, feats):
    y = 1 - place_ref[0] if dy else place_ref[0]
    c = 1 - place_ref[1] if dc else place_ref[1]
    return pl.ds(pl.multiple_of((y * 2 + c) * feats, feats), feats)


def out_part(x, near, far, place):
    nz, n, _ = x.shape
    depth, kv = near.shape
    steps = 2
    zs = nz // steps

    def kernel(place_ref, x_ref, near_ref, far_ref, out):
        y = place_ref[0]
        own = pl.ds(pl.multiple_of(y * depth, depth), depth)
        other = pl.ds(pl.multiple_of((1 - y) * depth, depth), depth)
        base = pl.program_id(0) * zs
        for z in range(0, zs, 2):
            total = jnp.zeros((2 * n, kv), F32)
            for cols, w_ref in ((own, near_ref), (other, far_ref)):
                block = jnp.concatenate([x_ref[base + z, :, cols], x_ref[base + z + 1, :, cols]], axis=0)
                total += jnp.dot(block, w_ref[...], preferred_element_type=F32)
            out[z] = total[:n].astype(BF16)
            out[z + 1] = total[n:].astype(BF16)

    return pl.pallas_call(
        kernel,
        grid=(steps,),
        in_specs=[SMEM] + [VMEM] * 3,
        out_specs=pl.BlockSpec((zs, n, kv), lambda g: (g, 0, 0)),
        out_shape=jax.ShapeDtypeStruct((nz, n, kv), BF16),
        compiler_params=pltpu.CompilerParams(vmem_limit_bytes=12 << 20),
        cost_estimate=pl.CostEstimate(flops=WAIT, bytes_accessed=4 << 20, transcendentals=0),
        name="out_part",
    )(place, x, near, far)


def grad_block(place_ref, x_ref, c_refs, turns, dy, dc, feats):
    cols = columns(place_ref, dy, dc, feats)
    nz = x_ref.shape[0]
    total = None
    at = 0
    for group in turns:
        refs, at = c_refs[at : at + len(group)], at + len(group)
        blocks = [x_ref[lax.rem(place_ref[2] - t + nz, nz), :, cols] for pair in group for t in pair]
        cots = refs[0][...] if len(refs) == 1 else jnp.concatenate([r[...] for r in refs], axis=0)
        part = lax.dot_general(jnp.concatenate(blocks, axis=0), cots, TURN, preferred_element_type=F32)
        total = part if total is None else total + part
    return total


def grad_part(name, x, cots, turns, place, feats, which, start, out_type, hint, after):
    kv = cots[0].shape[1]
    more = [] if start is None else [start]

    def kernel(place_ref, x_ref, *refs):
        out = refs[-1]
        for i, (dy, dc) in enumerate(which):
            total = grad_block(place_ref, x_ref, refs[: len(cots)], turns, dy, dc, feats)
            if more:
                total += refs[len(cots)][i]
            out[i] = total.astype(out_type)

    return call(
        name,
        kernel,
        [((len(which), feats, kv), out_type)],
        (place, x, *cots, *more, *after),
        [SMEM, VMEM] + [VMEM] * (len(cots) + len(more)) + [ANY] * len(after),
        flops=hint,
        moved=3 << 20,
    )[0]


def grad_far(kept, given):
    def kernel(kept_ref, given_ref, out):
        out[...] = (kept_ref[1] + given_ref[1].astype(F32)).astype(BF16)

    return call("grad_far", kernel, [(kept.shape[1:], BF16)], (kept, given), [VMEM] * 2, flops=kept.size)[0]


def momentum_step(kept, given, got, numer, moment, rep_tokens):
    g = kept + given.astype(F32) + got.astype(F32)
    v = MOMENT * moment + g * (1.0 / rep_tokens)
    return v, numer - LEARN * (g * (1.0 / rep_tokens) + MOMENT * v)


def push(kept, given, got, biased, momentum, weight, rep_tokens):
    size, kv = got.shape

    def kernel(w_ref, kept_ref, given_ref, got_ref, numer, moment, pushed):
        _, s = momentum_step(kept_ref[0], given_ref[0], got_ref[...], numer[0], moment[0], rep_tokens)
        pushed[:size] = s.astype(BF16)
        whole = jnp.full((TAIL, kv), w_ref[0], F32)
        high = whole.astype(BF16).astype(F32)
        middle = (whole - high).astype(BF16).astype(F32)
        low = whole - high - middle
        row = lax.broadcasted_iota(jnp.int32, (TAIL, kv), 0)
        pushed[size:] = jnp.where(row == 0, high, jnp.where(row == 1, middle, low)).astype(BF16)

    return call(
        "push",
        kernel,
        [((size + TAIL, kv), BF16)],
        (weight, kept, given, got, biased, momentum),
        [SMEM] + [VMEM] * 5,
        flops=8 * size * kv,
        moved=24 * size * kv,
    )[0]


def step(kept, given, got, biased, momentum, rep_tokens, after):
    size, kv = got.shape

    def kernel(_, kept_ref, given_ref, got_ref, numer, moment, velocity, stepped):
        v, s = momentum_step(kept_ref[0], given_ref[0], got_ref[...], numer[0], moment[0], rep_tokens)
        velocity[0] = v
        stepped[...] = s

    return call(
        "step",
        kernel,
        [((1, size, kv), F32), ((size, kv), F32)],
        (after, kept, given, got, biased, momentum),
        [ANY] + [VMEM] * 5,
        flops=0,
        moved=24 * size * kv,
    )


def mix(stepped, arrived, weight, after):
    size, kv = stepped.shape
    steps = 2

    def kernel(w_ref, _, s, a, tail, weight_out, mixed_out, debiased_out):
        parts = tail[...].astype(F32)
        w = 0.5 * (w_ref[0] + (parts[0:1] + parts[1:2] + parts[2:3]))
        weight_out[0] = w[0, 0]
        mixed = 0.5 * (s[...] + a[...].astype(F32))
        mixed_out[0] = mixed
        debiased_out[0] = mixed / w

    full = jax.ShapeDtypeStruct((1, size, kv), F32)
    piece = pl.BlockSpec((size // steps, kv), lambda g: (g, 0))
    piece_out = pl.BlockSpec((1, size // steps, kv), lambda g: (0, g, 0))
    return pl.pallas_call(
        kernel,
        grid=(steps,),
        in_specs=[SMEM, ANY, piece, piece, pl.BlockSpec((TAIL, kv), lambda g: (size // TAIL, 0))],
        out_specs=[SMEM, piece_out, piece_out],
        out_shape=[jax.ShapeDtypeStruct((1,), F32)] + [full] * 2,
        compiler_params=pltpu.CompilerParams(vmem_limit_bytes=12 << 20),
        cost_estimate=pl.CostEstimate(flops=6 * size * kv, bytes_accessed=22 * size * kv, transcendentals=0),
        name="mix",
    )(weight, after, stepped, arrived, arrived)


def sum_parts(parts):
    nz, rows, kv = parts.shape

    def kernel(parts_ref, out):
        total = parts_ref[0].astype(F32)
        for z in range(1, nz):
            total += parts_ref[z].astype(F32)
        out[...] = total.astype(BF16)

    return call("sum_parts", kernel, [((rows, kv), BF16)], (parts,), [VMEM], flops=parts.size, moved=2 * parts.size)[0]


def push_round(dist, tokens, own, biased, momentum, weight):
    ny, nz, nc = (lax.axis_size(a) for a in SHARD)
    feats = biased.shape[1]
    rep_tokens = own.shape[0] * ny * nz * nc
    swap = ((0, 1), (1, 0))
    n_rep = lax.axis_size("replica")
    ahead = [((i - dist) % n_rep, i) for i in range(n_rep)]
    place = jnp.stack([lax.axis_index(a) for a in ("yh", "core", "z")]).astype(jnp.int32)

    def along(block, turn):
        return lax.ppermute(block, "z", [(i, (i + turn) % nz) for i in range(nz)])

    pair, alone = join(own, along(own, 4))
    x = lax.all_to_all(pack(tokens, ny, nz), "z", 0, 0, tiled=True)
    first = [pair, along(alone, 2), along(alone, -2)]
    first_turns = [((0, 4),), ((2,), (6,))]
    last = [along(pair, 1), along(pair, -1)]
    last_turns = [((1, 5),), ((7, 3),)]

    near = lax.all_gather(rounded_rows(biased, weight, alone), "core", axis=0, tiled=True)
    far = lax.ppermute(near, "yh", swap)
    part = out_part(x, near, far, place)
    parts = lax.all_to_all(part, "z", 0, 0, tiled=True)

    mine, other = ((0, 0), (1, 0)), ((0, 1), (1, 1))
    start = grad_part("grad_first", x, first, first_turns, place, feats, other, None, F32, WAIT, [part])
    given = grad_part("grad_sent", x, last, last_turns, place, feats, other, start, BF16, 2 * WAIT, [])
    given = lax.ppermute(given, "core", swap)
    kept = grad_part("grad_kept", x, first + last, first_turns + last_turns, place, feats, mine, None, F32, 0, [])
    got = lax.ppermute(grad_far(kept, given), "yh", swap)
    output = sum_parts(parts)

    pushed = push(kept, given, got, biased, momentum, weight, rep_tokens)
    velocity, stepped = step(kept, given, got, biased, momentum, rep_tokens, pushed)
    arrived = lax.ppermute(pushed, "replica", ahead)
    weight_out, mixed, debiased = mix(stepped, arrived, weight, output)
    return output, mixed, weight_out, velocity, debiased


def shards(tokens, cotangent, biased, momentum, weight, round_index):
    hops = lax.axis_size("replica").bit_length() - 1
    power = round_index[0] % hops
    branches = [partial(push_round, 1 << level) for level in range(hops)]
    return lax.switch(power, branches, tokens, cotangent, biased, momentum, weight)


def solution(mesh):
    n_rep, n_shard = mesh.devices.shape
    inner = Mesh(mesh.devices.reshape(n_rep, 2, n_shard // 4, 2), ("replica",) + SHARD)
    rows = P(("replica",) + SHARD, None)
    held = P("replica", SHARD, None)
    return jax.shard_map(
        shards,
        mesh=inner,
        in_specs=(rows, rows, held, held, P("replica"), P()),
        out_specs=(rows, held, P("replica"), held, held),
        check_vma=False,
    )
```

```python
from functools import partial

import jax
import jax.numpy as jnp
from jax import lax
from jax.experimental import pallas as pl
from jax.experimental.pallas import tpu as pltpu
from jax.sharding import Mesh, PartitionSpec as P

MOMENT = 0.9
LEARN = 0.5
SHARD = ("yh", "z", "core")
F32, BF16 = jnp.float32, jnp.bfloat16
VMEM = pl.BlockSpec(memory_space=pltpu.VMEM)
SMEM = pl.BlockSpec(memory_space=pltpu.SMEM)
ANY = pl.BlockSpec(memory_space=pl.ANY)
TURN = (((0,), (0,)), ((), ()))
TAIL = 16
WAIT = 50_000_000_000


def call(name, kernel, outs, ins, specs, flops=0, moved=0, **kw):
    return pl.pallas_call(
        kernel,
        in_specs=specs,
        out_specs=[VMEM] * len(outs),
        out_shape=[jax.ShapeDtypeStruct(s, t) for s, t in outs],
        compiler_params=pltpu.CompilerParams(vmem_limit_bytes=12 << 20),
        cost_estimate=pl.CostEstimate(flops=flops, bytes_accessed=moved, transcendentals=0),
        name=name,
        **kw,
    )(*ins)


def rounded_rows(biased, weight, after):
    def kernel(weight_ref, _, numer, current):
        current[...] = (numer[0] / weight_ref[0]).astype(BF16)

    _, n, kv = biased.shape
    return call("rounded_rows", kernel, [((n, kv), BF16)], (weight, after, biased), [SMEM, ANY, VMEM])[0]


def pack(tokens, ny, nz):
    rows, width = tokens.shape
    steps = 2
    zs = nz // steps
    cols = width // ny // steps
    part = width // ny // nz

    def kernel(*refs):
        out = refs[-1]
        for p in range(zs):
            for y in range(ny):
                out[p, :, y * part : (y + 1) * part] = refs[y][:, p * part : (p + 1) * part]

    return pl.pallas_call(
        kernel,
        grid=(steps,),
        in_specs=[pl.BlockSpec((rows, cols), lambda g, y=y: (0, y * steps + g)) for y in range(ny)],
        out_specs=pl.BlockSpec((zs, rows, ny * part), lambda g: (g, 0, 0)),
        out_shape=jax.ShapeDtypeStruct((nz, rows, ny * part), BF16),
        compiler_params=pltpu.CompilerParams(vmem_limit_bytes=60 << 20),
        cost_estimate=pl.CostEstimate(flops=0, bytes_accessed=4 * rows * width, transcendentals=0),
        name="pack",
    )(*[tokens] * ny)


def join(first, second):
    n, kv = first.shape

    def kernel(first_ref, second_ref, out, alone):
        out[:n] = first_ref[...]
        out[n:] = second_ref[...]
        alone[...] = first_ref[...]

    outs = [((2 * n, kv), BF16), ((n, kv), BF16)]
    return call("join", kernel, outs, (first, second), [VMEM] * 2, flops=WAIT)


def columns(place_ref, dy, dc, feats):
    y = 1 - place_ref[0] if dy else place_ref[0]
    c = 1 - place_ref[1] if dc else place_ref[1]
    return pl.ds(pl.multiple_of((y * 2 + c) * feats, feats), feats)


def out_part(x, near, far, place):
    nz, n, _ = x.shape
    depth, kv = near.shape
    steps = 2
    zs = nz // steps

    def kernel(place_ref, x_ref, near_ref, far_ref, out):
        y = place_ref[0]
        own = pl.ds(pl.multiple_of(y * depth, depth), depth)
        other = pl.ds(pl.multiple_of((1 - y) * depth, depth), depth)
        base = pl.program_id(0) * zs
        for z in range(0, zs, 2):
            total = jnp.zeros((2 * n, kv), F32)
            for cols, w_ref in ((own, near_ref), (other, far_ref)):
                block = jnp.concatenate([x_ref[base + z, :, cols], x_ref[base + z + 1, :, cols]], axis=0)
                total += jnp.dot(block, w_ref[...], preferred_element_type=F32)
            out[z] = total[:n].astype(BF16)
            out[z + 1] = total[n:].astype(BF16)

    return pl.pallas_call(
        kernel,
        grid=(steps,),
        in_specs=[SMEM] + [VMEM] * 3,
        out_specs=pl.BlockSpec((zs, n, kv), lambda g: (g, 0, 0)),
        out_shape=jax.ShapeDtypeStruct((nz, n, kv), BF16),
        compiler_params=pltpu.CompilerParams(vmem_limit_bytes=12 << 20),
        cost_estimate=pl.CostEstimate(flops=WAIT, bytes_accessed=4 << 20, transcendentals=0),
        name="out_part",
    )(place, x, near, far)


def grad_block(place_ref, x_ref, c_refs, turns, dy, dc, feats):
    cols = columns(place_ref, dy, dc, feats)
    nz = x_ref.shape[0]
    total = None
    at = 0
    for group in turns:
        refs, at = c_refs[at : at + len(group)], at + len(group)
        blocks = [x_ref[lax.rem(place_ref[2] - t + nz, nz), :, cols] for pair in group for t in pair]
        cots = refs[0][...] if len(refs) == 1 else jnp.concatenate([r[...] for r in refs], axis=0)
        part = lax.dot_general(jnp.concatenate(blocks, axis=0), cots, TURN, preferred_element_type=F32)
        total = part if total is None else total + part
    return total


def grad_part(name, x, cots, turns, place, feats, which, start, out_type, hint, after):
    kv = cots[0].shape[1]
    more = [] if start is None else [start]

    def kernel(place_ref, x_ref, *refs):
        out = refs[-1]
        for i, (dy, dc) in enumerate(which):
            total = grad_block(place_ref, x_ref, refs[: len(cots)], turns, dy, dc, feats)
            if more:
                total += refs[len(cots)][i]
            out[i] = total.astype(out_type)

    return call(
        name,
        kernel,
        [((len(which), feats, kv), out_type)],
        (place, x, *cots, *more, *after),
        [SMEM, VMEM] + [VMEM] * (len(cots) + len(more)) + [ANY] * len(after),
        flops=hint,
        moved=3 << 20,
    )[0]


def grad_far(kept, given):
    def kernel(kept_ref, given_ref, out):
        out[...] = (kept_ref[1] + given_ref[1].astype(F32)).astype(BF16)

    return call("grad_far", kernel, [(kept.shape[1:], BF16)], (kept, given), [VMEM] * 2, flops=kept.size)[0]


def momentum_step(kept, given, got, numer, moment, rep_tokens):
    g = kept + given.astype(F32) + got.astype(F32)
    v = MOMENT * moment + g * (1.0 / rep_tokens)
    return v, numer - LEARN * (g * (1.0 / rep_tokens) + MOMENT * v)


def push(kept, given, got, biased, momentum, weight, rep_tokens):
    size, kv = got.shape

    def kernel(w_ref, kept_ref, given_ref, got_ref, numer, moment, pushed):
        _, s = momentum_step(kept_ref[0], given_ref[0], got_ref[...], numer[0], moment[0], rep_tokens)
        pushed[:size] = s.astype(BF16)
        whole = jnp.full((TAIL, kv), w_ref[0], F32)
        high = whole.astype(BF16).astype(F32)
        middle = (whole - high).astype(BF16).astype(F32)
        low = whole - high - middle
        row = lax.broadcasted_iota(jnp.int32, (TAIL, kv), 0)
        pushed[size:] = jnp.where(row == 0, high, jnp.where(row == 1, middle, low)).astype(BF16)

    return call(
        "push",
        kernel,
        [((size + TAIL, kv), BF16)],
        (weight, kept, given, got, biased, momentum),
        [SMEM] + [VMEM] * 5,
        flops=8 * size * kv,
        moved=24 * size * kv,
    )[0]


def step(kept, given, got, biased, momentum, rep_tokens, after):
    size, kv = got.shape

    def kernel(_, kept_ref, given_ref, got_ref, numer, moment, velocity, stepped):
        v, s = momentum_step(kept_ref[0], given_ref[0], got_ref[...], numer[0], moment[0], rep_tokens)
        velocity[0] = v
        stepped[...] = s

    return call(
        "step",
        kernel,
        [((1, size, kv), F32), ((size, kv), F32)],
        (after, kept, given, got, biased, momentum),
        [ANY] + [VMEM] * 5,
        flops=0,
        moved=24 * size * kv,
    )


def mix(stepped, arrived, weight, after):
    size, kv = stepped.shape
    steps = 2

    def kernel(w_ref, _, s, a, tail, weight_out, mixed_out, debiased_out):
        parts = tail[...].astype(F32)
        w = 0.5 * (w_ref[0] + (parts[0:1] + parts[1:2] + parts[2:3]))
        weight_out[0] = w[0, 0]
        mixed = 0.5 * (s[...] + a[...].astype(F32))
        mixed_out[0] = mixed
        debiased_out[0] = mixed / w

    full = jax.ShapeDtypeStruct((1, size, kv), F32)
    piece = pl.BlockSpec((size // steps, kv), lambda g: (g, 0))
    piece_out = pl.BlockSpec((1, size // steps, kv), lambda g: (0, g, 0))
    return pl.pallas_call(
        kernel,
        grid=(steps,),
        in_specs=[SMEM, ANY, piece, piece, pl.BlockSpec((TAIL, kv), lambda g: (size // TAIL, 0))],
        out_specs=[SMEM, piece_out, piece_out],
        out_shape=[jax.ShapeDtypeStruct((1,), F32)] + [full] * 2,
        compiler_params=pltpu.CompilerParams(vmem_limit_bytes=12 << 20),
        cost_estimate=pl.CostEstimate(flops=6 * size * kv, bytes_accessed=22 * size * kv, transcendentals=0),
        name="mix",
    )(weight, after, stepped, arrived, arrived)


def sum_parts(parts):
    nz, rows, kv = parts.shape

    def kernel(parts_ref, out):
        total = parts_ref[0].astype(F32)
        for z in range(1, nz):
            total += parts_ref[z].astype(F32)
        out[...] = total.astype(BF16)

    return call("sum_parts", kernel, [((rows, kv), BF16)], (parts,), [VMEM], flops=parts.size, moved=2 * parts.size)[0]


def push_round(dist, tokens, own, biased, momentum, weight):
    ny, nz, nc = (lax.axis_size(a) for a in SHARD)
    feats = biased.shape[1]
    rep_tokens = own.shape[0] * ny * nz * nc
    swap = ((0, 1), (1, 0))
    n_rep = lax.axis_size("replica")
    ahead = [((i - dist) % n_rep, i) for i in range(n_rep)]
    place = jnp.stack([lax.axis_index(a) for a in ("yh", "core", "z")]).astype(jnp.int32)

    def along(block, turn):
        return lax.ppermute(block, "z", [(i, (i + turn) % nz) for i in range(nz)])

    pair, alone = join(own, along(own, 4))
    x = lax.all_to_all(pack(tokens, ny, nz), "z", 0, 0, tiled=True)
    first = [pair, along(alone, 2), along(alone, -2)]
    first_turns = [((0, 4),), ((2,), (6,))]
    last = [along(pair, 1), along(pair, -1)]
    last_turns = [((1, 5),), ((7, 3),)]

    near = lax.all_gather(rounded_rows(biased, weight, alone), "core", axis=0, tiled=True)
    far = lax.ppermute(near, "yh", swap)
    part = out_part(x, near, far, place)
    parts = lax.all_to_all(part, "z", 0, 0, tiled=True)

    mine, other = ((0, 0), (1, 0)), ((0, 1), (1, 1))
    start = grad_part("grad_first", x, first, first_turns, place, feats, other, None, F32, WAIT, [part])
    given = grad_part("grad_sent", x, last, last_turns, place, feats, other, start, BF16, 2 * WAIT, [])
    given = lax.ppermute(given, "core", swap)
    kept = grad_part("grad_kept", x, first + last, first_turns + last_turns, place, feats, mine, None, F32, 0, [])
    got = lax.ppermute(grad_far(kept, given), "yh", swap)
    output = sum_parts(parts)

    pushed = push(kept, given, got, biased, momentum, weight, rep_tokens)
    velocity, stepped = step(kept, given, got, biased, momentum, rep_tokens, pushed)
    arrived = lax.ppermute(pushed, "replica", ahead)
    weight_out, mixed, debiased = mix(stepped, arrived, weight, output)
    return output, mixed, weight_out, velocity, debiased


def shards(tokens, cotangent, biased, momentum, weight, round_index):
    hops = lax.axis_size("replica").bit_length() - 1
    power = round_index[0] & (hops - 1)
    branches = [partial(push_round, 1 << level) for level in range(hops)]
    return lax.switch(power, branches, tokens, cotangent, biased, momentum, weight)


def solution(mesh):
    n_rep, n_shard = mesh.devices.shape
    inner = Mesh(mesh.devices.reshape(n_rep, 2, n_shard // 4, 2), ("replica",) + SHARD)
    rows = P(("replica",) + SHARD, None)
    held = P("replica", SHARD, None)
    return jax.shard_map(
        shards,
        mesh=inner,
        in_specs=(rows, rows, held, held, P("replica"), P()),
        out_specs=(rows, held, P("replica"), held, held),
        check_vma=False,
    )
```
